256 devices in a mesh: gx: 128 (over x_lo, y, z, core), gy: 2 (over x_hi).
Axes of the slice: x: 4 (x_hi: 2, x_lo: 2; x = x_hi * 2 + x_lo), y: 4, z: 8, core: 2. Of those that a mesh axis runs over, the one named last changes fastest.
Arguments:
- velocity: float32 [3, 512, 32, 128], P(None, 'gx', 'gy'), may hold values from -6 to 6
- kernel_in: bfloat16 [64, 3, 3, 3, 3], replicated, may hold values from -0.625 to 0.625
- kernel_mid: bfloat16 [64, 64, 3, 3, 3], replicated, may hold values from -0.15625 to 0.15625
- kernel_out: bfloat16 [6, 64, 3, 3, 3], replicated, may hold values from -0.15625 to 0.15625
Outputs:
- tendency: float32 [3, 512, 32, 128], P(None, 'gx', 'gy')
- stress: float32 [6, 512, 32, 128], P(None, 'gx', 'gy')
The draws below stay inside these ranges and needn't reach their ends.
All inputs are finite; a program needn't handle non-finite values.
Results may differ from the reference program's by a relative error of at most 0.0056.
Values may be sent and summed in bfloat16 or wider, within the bound.
A program may use at most 128 MiB of HBM per device.

```python
import jax
import jax.numpy as jnp
from jax import lax

CX = 4
NZ = 128
CH = 64
NX = 512
NY = 32
N_GX = 128


def steps_of(stream_key, extent, cuts, smallest, high):
    def one(dim, shards_of):
        steps = jax.random.uniform(jax.random.fold_in(jax.random.fold_in(stream_key, 6), dim), (shards_of,), jnp.float32, smallest / len(cuts), high / len(cuts))
        return jnp.repeat(jnp.exp(steps), extent[dim] // shards_of).reshape((-1,) + (1,) * (len(extent) - dim - 1))

    factor_of = one(*cuts[0])
    for cut in cuts[1:]:
        factor_of = factor_of * one(*cut)
    return factor_of


def bell_draw(rng, extent, spread, most, cuts=(), kind=jnp.bfloat16):
    values = jax.random.normal(rng, extent, jnp.float32) * spread
    if len(cuts) > 0:
        values = steps_of(rng, extent, cuts, -0.22, 0.18) * values
    return jnp.clip(values, min=-most, max=most).astype(kind)


def setup_inputs(seed: int = 0) -> dict:
    streams_of = jax.random.split(jax.random.key(seed), 5)
    return {
        "velocity": bell_draw(streams_of[0], (3, NX, NY, NZ), 1.0, 6.0, ((1, 128), (2, 2)), jnp.float32),
        "kernel_in": bell_draw(streams_of[1], (CH, 3, 3, 3, 3), 81 ** -0.5, 0.625),
        "kernel_mid": bell_draw(streams_of[2], (CH, CH, 3, 3, 3), (27 * CH) ** -0.5, 0.15625),
        "kernel_out": bell_draw(streams_of[3], (6, CH, 3, 3, 3), (27 * CH) ** -0.5, 0.15625),
    }


FIRST = ((1, 0.75), (2, -0.15), (3, 1.0 / 60.0))
SECOND = ((1, 1.5), (2, -0.15), (3, 1.0 / 90.0))
CENTER = -49.0 / 18.0


def extend(field, rim):
    wrapped = jnp.pad(field, ((0, 0), (rim, rim), (0, 0), (0, 0)), mode="wrap")
    return jnp.pad(wrapped, ((0, 0), (0, 0), (rim, rim), (0, 0)))


def cut(ext, axis, start, count):
    return lax.slice_in_dim(ext, start, start + count, axis=axis)


def first_deriv(ext, axis, count):
    total = 0.0
    for step, coef in FIRST:
        total = total + coef * (cut(ext, axis, 3 + step, count) - cut(ext, axis, 3 - step, count))
    return total


def second_deriv(ext, axis, count):
    total = CENTER * cut(ext, axis, 3, count)
    for step, coef in SECOND:
        total = total + coef * (cut(ext, axis, 3 + step, count) + cut(ext, axis, 3 - step, count))
    return total


def first_span(field):
    total = 0.0
    for step, coef in FIRST:
        total = total + coef * (jnp.roll(field, -step, 3) - jnp.roll(field, step, 3))
    return total


def second_span(field):
    total = CENTER * field
    for step, coef in SECOND:
        total = total + coef * (jnp.roll(field, -step, 3) + jnp.roll(field, step, 3))
    return total


def layer(act, kernel):
    wide = jnp.pad(act.astype(jnp.float32), ((0, 0), (0, 0), (1, 1), (0, 0)))
    wide = jnp.concatenate([wide[..., -1:], wide, wide[..., :1]], axis=3)
    out = lax.conv_general_dilated(wide[None], kernel.astype(jnp.float32), (1, 1, 1), "VALID",
                                   dimension_numbers=("NCDHW", "OIDHW", "NCDHW"),
                                   precision=lax.Precision.HIGHEST)
    return out[0]


def reference(velocity, kernel_in, kernel_mid, kernel_out):
    vel16 = velocity.astype(jnp.bfloat16)
    padded = jnp.pad(vel16, ((0, 0), (3, 3), (0, 0), (0, 0)), mode="wrap")

    def closure(start):
        piece = lax.dynamic_slice_in_dim(padded, start, CX + 6, axis=1)
        hidden1 = jax.nn.gelu(layer(piece, kernel_in), approximate=True).astype(jnp.bfloat16)
        hidden2 = jax.nn.gelu(layer(hidden1, kernel_mid), approximate=True).astype(jnp.bfloat16)
        return layer(hidden2, kernel_out)

    starts = jnp.arange(N_GX, dtype=jnp.int32) * CX
    blocks = lax.map(closure, starts)
    stress = jnp.transpose(blocks, (1, 0, 2, 3, 4)).reshape(6, NX, NY, NZ)

    vel_ext = extend(velocity, 3)
    ext_x = vel_ext[:, :, 3:-3, :]
    ext_y = vel_ext[:, 3:-3, :, :]
    grad_x = first_deriv(ext_x, 1, NX)
    grad_y = first_deriv(ext_y, 2, NY)
    grad_z = first_span(velocity)
    advect = velocity[0][None] * grad_x + velocity[1][None] * grad_y + velocity[2][None] * grad_z
    lap = second_deriv(ext_x, 1, NX) + second_deriv(ext_y, 2, NY) + second_span(velocity)

    str_ext = extend(stress, 3)
    parts_x = jnp.stack([str_ext[0], str_ext[3], str_ext[4]])[:, :, 3:-3, :]
    parts_y = jnp.stack([str_ext[3], str_ext[1], str_ext[5]])[:, 3:-3, :, :]
    parts_z = jnp.stack([stress[4], stress[5], stress[2]])
    divergence = first_deriv(parts_x, 1, NX) + first_deriv(parts_y, 2, NY) + first_span(parts_z)
    tendency = -advect + 0.2 * lap - divergence
    return tendency, stress
```

```python
import functools
import math

import jax
import jax.numpy as jnp
from jax import lax
from jax.experimental import pallas as pl
from jax.experimental.pallas import tpu as pltpu
from jax.sharding import PartitionSpec as P

MESH = pl.DeviceIdType.MESH
F32 = jnp.float32
BF16 = jnp.bfloat16

A1 = (0.75, -0.15, 1.0 / 60.0)
A2 = (1.5, -0.15, 1.0 / 90.0)
CENTER = -49.0 / 18.0
G0 = math.sqrt(2.0 / math.pi)
G1 = G0 * 0.044715

ORDER = (0, 4, 3, 1, 5, 2)
URO = 20 * 16


def gelu(s):
    half = 0.5 * s
    return half + half * jnp.tanh(s * (G0 + G1 * (s * s)))


def spin(a, k):
    return pltpu.roll(a, k % 128, 1)


def band(w0, w1, w2):
    zero = jnp.zeros_like(w0)
    cat = lambda a, b: jnp.concatenate([a, b], axis=1)
    return cat(w0, w1), cat(w2, zero), cat(zero, w0), cat(w1, w2)


def kernel(
    vel_hbm, wi_hbm, wm_hbm, wo_hbm, ten_ref, str_ref,
    v, hx, hy, ysend, uf, u16, wi_raw, wm_raw, wo_raw, wt0, wt1, wi, wp, wof, wo, h1, h2, q, ve, s, s16, ys16, sx, sy, se,
    load_sem, send_a, recv_a, send_b, recv_b,
):
    n = 128
    gx = lax.axis_index("gx")
    gy = lax.axis_index("gy")
    lo = lax.rem(gx + n - 1, n)
    hi = lax.rem(gx + 1, n)
    oy = 1 - gy
    peers = ((lo, gy), (hi, gy), (gx, oy), (lo, oy), (hi, oy))
    opposite = (1, 0, 2, 4, 3)

    barrier = pltpu.get_barrier_semaphore()
    for peer in peers:
        pl.semaphore_signal(barrier, inc=1, device_id=peer, device_id_type=MESH)
    loads = [
        pltpu.make_async_copy(vel_hbm, v.at[pl.ds(0, 192)], load_sem.at[0]),
        pltpu.make_async_copy(wi_hbm, wi_raw, load_sem.at[1]),
        pltpu.make_async_copy(wm_hbm, wm_raw, load_sem.at[2]),
        pltpu.make_async_copy(wo_hbm, wo_raw, load_sem.at[3]),
    ]
    for load in loads:
        load.start()
    v[pl.ds(192, 64), :] = jnp.zeros((64, 128), F32)
    loads[0].wait()
    near = 13 * (1 - gy)
    for r in range(3):
        ysend[r] = v[pl.ds(near + r, 16, stride=16), :]
    pl.semaphore_wait(barrier, 5)

    v3 = v.at[pl.ds(0, 192)].reshape(3, 64, 128)
    sends = []
    for k in range(5):
        if k == 0:
            src, dst = v3.at[:, pl.ds(0, 48), :], hx.at[opposite[k]]
        elif k == 1:
            src, dst = v3.at[:, pl.ds(16, 48), :], hx.at[opposite[k]]
        else:
            src, dst = ysend, hy.at[opposite[k] - 2]
        sends.append(
            pltpu.make_async_remote_copy(
                src_ref=src, dst_ref=dst, send_sem=send_a.at[k], recv_sem=recv_a.at[opposite[k]],
                device_id=peers[k], device_id_type=MESH,
            )
        )
        sends[-1].start()

    @pl.loop(0, 10)
    def _(i):
        uf[pl.ds(i * URO, URO), :] = jnp.zeros((URO, 128), F32)

    def patch(field, x, c):
        for dz in range(3):
            start = x * URO + (2 * gy + 1) * 16 + dz * 3 + c
            uf[pl.ds(start, 16, stride=16), :] = spin(field, 1 - dz)

    for c in range(3):
        for x in range(4):
            patch(v[pl.ds((c * 4 + x) * 16, 16), :], x + 3, c)

    loads[1].wait()
    wt0[...] = jnp.zeros_like(wt0)
    wt1[...] = jnp.zeros_like(wt1)
    for c in range(3):
        for dx in range(3):
            for dy in range(3):
                w = wi_raw[c, dx, dy].astype(F32)
                wide = jnp.concatenate([w, jnp.zeros_like(w)], axis=1)
                row = dx * 48 + dy * 16 + c
                wt0[pl.ds(row, 3, stride=3), :] = wide
                wt1[pl.ds(row + 48, 3, stride=3), :] = spin(wide, 64)
    wi[...] = (wt0[...] + wt1[...]).T[:, :192].astype(BF16)

    loads[2].wait()
    for dy in range(3):
        for dz in range(3):
            a, b, c, d = band(wm_raw[0, dy, dz], wm_raw[1, dy, dz], wm_raw[2, dy, dz])
            wp[pl.ds(dz * 128, 64), pl.ds(dy * 256, 128)] = a
            wp[pl.ds(dz * 128, 64), pl.ds(dy * 256 + 128, 128)] = b
            wp[pl.ds(dz * 128 + 64, 64), pl.ds(dy * 256, 128)] = c
            wp[pl.ds(dz * 128 + 64, 64), pl.ds(dy * 256 + 128, 128)] = d

    loads[3].wait()
    wof[...] = jnp.zeros_like(wof)
    for k in range(6):
        for dy in range(3):
            a, b, c, d = band(*(wo_raw[ORDER[k], dx, dy].astype(F32) for dx in range(3)))
            for x in range(4):
                first, second = ((a, b), (c, d))[x % 2]
                rows = pl.ds(dy * 72 + k * 4 + x, 3, stride=24)
                wof[x // 2, rows, :] = first
                wof[x // 2 + 1, rows, :] = second
    for m in range(3):
        wo[:, pl.ds(m * 128, 128)] = wof[m].astype(BF16)

    h1[0] = jnp.zeros((512, 128), BF16)
    h1[19] = jnp.zeros((512, 128), BF16)
    for dy in range(3):
        q[dy, 0] = jnp.zeros((24, 128), F32)
        q[dy, 19] = jnp.zeros((24, 128), F32)

    for k in range(5):
        sends[k].wait_recv()

    for c in range(3):
        for x in range(3):
            patch(hx[0, c, pl.ds(x * 16, 16), :], x, c)
            patch(hx[1, c, pl.ds(x * 16, 16), :], x + 7, c)
    far = jnp.where(gy == 0, 17, 0)
    for r in range(3):
        for side, x_from, x_to, count in ((0, 0, 3, 4), (1, 1, 0, 3), (2, 0, 7, 3)):
            row = hy[side, r]
            for dz in range(3):
                turned = spin(row, 1 - dz)
                for c in range(3):
                    start = x_to * URO + (far + r) * 16 + dz * 3 + c
                    uf[pl.ds(start, count, stride=URO), :] = turned[c * 4 + x_from:c * 4 + x_from + count]

    @pl.loop(0, 10)
    def _(i):
        u16[pl.ds(i * URO, URO), :] = uf[pl.ds(i * URO, URO), :].astype(BF16)

    @pl.loop(0, 9)
    def _(t):
        j = t * 2
        for p in range(4):
            def rows(dj):
                return jnp.concatenate(
                    [u16[pl.ds((2 * p + i) * URO + (j + dj) * 16, 48), :] for i in range(4)], axis=0
                )
            out = gelu(jnp.dot(wi[...], jnp.concatenate([rows(0), rows(1)], axis=1), preferred_element_type=F32))
            out = out.astype(BF16)
            h1[j + 1, pl.ds(p * 128, 128), :] = out[:, :128]
            h1[j + 2, pl.ds(p * 128, 128), :] = out[:, 128:]

    @pl.loop(0, 9)
    def _(t):
        j = t * 2
        for p in range(3):
            def rows(dj):
                return jnp.concatenate(
                    [h1[j + dj + dy, pl.ds(p * 128, 256), :] for dy in range(3)], axis=0
                )
            part = jnp.dot(wp[...], jnp.concatenate([rows(0), rows(1)], axis=1), preferred_element_type=F32)
            for dj in range(2):
                half = part[:, dj * 128:dj * 128 + 128]
                out = gelu(spin(half[0:128], 1) + half[128:256] + spin(half[256:384], -1))
                h2[j + dj, pl.ds(p * 128, 128), :] = out.astype(BF16)

    @pl.loop(0, 9)
    def _(t):
        j = t * 2
        part = jnp.dot(wo[...], jnp.concatenate([h2[j], h2[j + 1]], axis=1), preferred_element_type=F32)
        for dj in range(2):
            half = part[:, dj * 128:dj * 128 + 128]
            for dy in range(3):
                at = dy * 72
                q[dy, j + dj + 1] = (
                    spin(half[at:at + 24], 1) + half[at + 24:at + 48] + spin(half[at + 48:at + 72], -1)
                )

    @pl.loop(0, 16)
    def _(y):
        j = y + 2 * gy
        s[pl.ds(y, 24, stride=16), :] = q[0, j] + q[1, j + 1] + q[2, j + 2]

    for k in range(3):
        s16[k] = s[pl.ds(k * 64, 64), :].astype(BF16)
    for r in range(3):
        ys16[r] = s[pl.ds(128 + near + r, 16, stride=16), :].astype(BF16)
    last = []
    for k in range(3):
        if k == 0:
            src, dst = s16.at[:, pl.ds(0, 48), :], sx.at[1]
        elif k == 1:
            src, dst = s16.at[:, pl.ds(16, 48), :], sx.at[0]
        else:
            src, dst = ys16, sy
        last.append(
            pltpu.make_async_remote_copy(
                src_ref=src, dst_ref=dst, send_sem=send_b.at[k], recv_sem=recv_b.at[opposite[k]],
                device_id=peers[k], device_id_type=MESH,
            )
        )
        last[-1].start()

    low_side = gy == 1

    def edge(ext, halo, count):
        for r in range(3):
            row = halo(r)
            ext[pl.ds(24 + r, count, stride=32), :] = jnp.where(low_side, 0.0, row)
            ext[pl.ds(5 + r, count, stride=32), :] = jnp.where(low_side, row, 0.0)

    def x_plane(c, x):
        if x < 0:
            return hx[0, c, pl.ds((x + 3) * 16, 16), :]
        if x > 3:
            return hx[1, c, pl.ds((x - 4) * 16, 16), :]
        return v[pl.ds((c * 4 + x) * 16, 16), :]

    for i in range(12):
        ve[pl.ds(i * 32 + 8, 16), :] = v[pl.ds(i * 16, 16), :]
    edge(ve, lambda r: hy[0, r, pl.ds(0, 12), :], 12)
    for c in range(3):
        for x in range(4):
            mid = x_plane(c, x)
            base = (c * 4 + x) * 32 + 8
            d1 = [0.0, 0.0, 0.0]
            d2 = (3.0 * CENTER) * mid
            for k in range(3):
                pairs = (
                    (x_plane(c, x + k + 1), x_plane(c, x - k - 1)),
                    (ve[pl.ds(base + k + 1, 16), :], ve[pl.ds(base - k - 1, 16), :]),
                    (spin(mid, -k - 1), spin(mid, k + 1)),
                )
                for a, (up, down) in enumerate(pairs):
                    d1[a] = d1[a] + A1[k] * (up - down)
                    d2 = d2 + A2[k] * (up + down)
            advect = x_plane(0, x) * d1[0] + x_plane(1, x) * d1[1] + x_plane(2, x) * d1[2]
            ten_ref[pl.ds((c * 4 + x) * 16, 16), :] = 0.2 * d2 - advect
    for k in range(6):
        str_ref[pl.ds(ORDER[k] * 64, 64), :] = s[pl.ds(k * 64, 64), :]
    for i in range(12):
        se[pl.ds(i * 32 + 8, 16), :] = s[pl.ds(128 + i * 16, 16), :]

    for k in range(3):
        last[k].wait_recv()

    def s_plane(k, x):
        if x < 0:
            return sx[0, k, pl.ds((x + 3) * 16, 16), :].astype(F32)
        if x > 3:
            return sx[1, k, pl.ds((x - 4) * 16, 16), :].astype(F32)
        return s[pl.ds((k * 4 + x) * 16, 16), :]

    edge(se, lambda r: sy[r].astype(F32)[:12], 12)
    for c, (along_x, along_y, along_z) in enumerate(((0, 0, 1), (2, 1, 4), (1, 2, 5))):
        for x in range(4):
            base = (along_y * 4 + x) * 32 + 8
            mid = s[pl.ds((along_z * 4 + x) * 16, 16), :]
            total = ten_ref[pl.ds((c * 4 + x) * 16, 16), :]
            for k in range(3):
                total = total - A1[k] * (
                    (s_plane(along_x, x + k + 1) - s_plane(along_x, x - k - 1))
                    + (se[pl.ds(base + k + 1, 16), :] - se[pl.ds(base - k - 1, 16), :])
                    + (spin(mid, -k - 1) - spin(mid, k + 1))
                )
            ten_ref[pl.ds((c * 4 + x) * 16, 16), :] = total

    for send in sends + last:
        send.wait_send()


def shards(velocity, kernel_in, kernel_mid, kernel_out):
    anywhere = pl.BlockSpec(memory_space=pl.ANY)
    whole = pl.BlockSpec(memory_space=pltpu.VMEM)
    tendency, stress = pl.pallas_call(
        kernel,
        out_shape=(jax.ShapeDtypeStruct((192, 128), F32), jax.ShapeDtypeStruct((384, 128), F32)),
        in_specs=[anywhere] * 4,
        out_specs=(whole, whole),
        scratch_shapes=[
            pltpu.VMEM((256, 128), F32),
            pltpu.VMEM((2, 3, 48, 128), F32),
            pltpu.VMEM((3, 3, 16, 128), F32),
            pltpu.VMEM((3, 16, 128), F32),
            pltpu.VMEM((10 * URO, 128), F32),
            pltpu.VMEM((10 * URO, 128), BF16),
            pltpu.VMEM((3, 3, 3, 3, 64), BF16),
            pltpu.VMEM((3, 3, 3, 64, 64), BF16),
            pltpu.VMEM((6, 3, 3, 3, 64), BF16),
            pltpu.VMEM((256, 128), F32),
            pltpu.VMEM((256, 128), F32),
            pltpu.VMEM((128, 192), BF16),
            pltpu.VMEM((384, 768), BF16),
            pltpu.VMEM((3, 216, 128), F32),
            pltpu.VMEM((216, 384), BF16),
            pltpu.VMEM((20, 512, 128), BF16),
            pltpu.VMEM((18, 384, 128), BF16),
            pltpu.VMEM((3, 20, 24, 128), F32),
            pltpu.VMEM((12 * 32, 128), F32),
            pltpu.VMEM((384, 128), F32),
            pltpu.VMEM((3, 64, 128), BF16),
            pltpu.VMEM((3, 16, 128), BF16),
            pltpu.VMEM((2, 3, 48, 128), BF16),
            pltpu.VMEM((3, 16, 128), BF16),
            pltpu.VMEM((12 * 32, 128), F32),
            pltpu.SemaphoreType.DMA((4,)),
            pltpu.SemaphoreType.DMA((5,)),
            pltpu.SemaphoreType.DMA((5,)),
            pltpu.SemaphoreType.DMA((3,)),
            pltpu.SemaphoreType.DMA((3,)),
        ],
        compiler_params=pltpu.CompilerParams(
            collective_id=0, has_side_effects=True, vmem_limit_bytes=48 * 1024 * 1024
        ),
    )(
        velocity.reshape(192, 128),
        jnp.transpose(kernel_in, (1, 2, 3, 4, 0)),
        jnp.transpose(kernel_mid, (2, 3, 4, 0, 1)),
        jnp.transpose(kernel_out, (0, 2, 3, 4, 1)),
    )
    return tendency.reshape(3, 4, 16, 128), stress.reshape(6, 4, 16, 128)


def solution(mesh):
    placed = (P(None, "gx", "gy", None), P(), P(), P())
    return jax.shard_map(
        shards,
        mesh=mesh,
        in_specs=placed,
        out_specs=(P(None, "gx", "gy", None), P(None, "gx", "gy", None)),
        check_vma=False,
    )
```

```python
import functools
import math

import jax
import jax.numpy as jnp
from jax import lax
from jax.experimental import pallas as pl
from jax.experimental.pallas import tpu as pltpu
from jax.sharding import PartitionSpec as P

MESH = pl.DeviceIdType.MESH
F32 = jnp.float32
BF16 = jnp.bfloat16

A1 = (0.75, -0.15, 1.0 / 60.0)
A2 = (1.5, -0.15, 1.0 / 90.0)
CENTER = -49.0 / 18.0
G0 = math.sqrt(2.0 / math.pi)
G1 = G0 * 0.044715

ORDER = (0, 4, 3, 1, 5, 2)
URO = 20 * 16


def gelu(s):
    half = 0.5 * s
    return half + half * jnp.tanh(s * (G0 + G1 * (s * s)))


def spin(a, k):
    return pltpu.roll(a, k % 128, 1)


def band(w0, w1, w2):
    zero = jnp.zeros_like(w0)
    cat = lambda a, b: jnp.concatenate([a, b], axis=1)
    return cat(w0, w1), cat(w2, zero), cat(zero, w0), cat(w1, w2)


def kernel(
    vel_hbm, wi_hbm, wm_hbm, wo_hbm, ten_ref, str_ref,
    v, hx, hy, hd, ysend, ydiag, uf, u16, wi_raw, wm_raw, wo_raw, wt0, wt1, wi, wp, wof, wo, h1, h2, q, ve, s, s16, ys16, sx, sy, se,
    load_sem, send_a, recv_a, send_b, recv_b,
):
    n = 128
    gx = lax.axis_index("gx")
    gy = lax.axis_index("gy")
    lo = lax.rem(gx + n - 1, n)
    hi = lax.rem(gx + 1, n)
    oy = 1 - gy
    peers = ((lo, gy), (hi, gy), (gx, oy), (lo, oy), (hi, oy))
    opposite = (1, 0, 2, 4, 3)

    barrier = pltpu.get_barrier_semaphore()
    for peer in peers:
        pl.semaphore_signal(barrier, inc=1, device_id=peer, device_id_type=MESH)
    loads = [
        pltpu.make_async_copy(vel_hbm, v.at[pl.ds(0, 192)], load_sem.at[0]),
        pltpu.make_async_copy(wi_hbm, wi_raw, load_sem.at[1]),
        pltpu.make_async_copy(wm_hbm, wm_raw, load_sem.at[2]),
        pltpu.make_async_copy(wo_hbm, wo_raw, load_sem.at[3]),
    ]
    for load in loads:
        load.start()
    v[pl.ds(192, 64), :] = jnp.zeros((64, 128), F32)

    def remote(src, dst, k, send_sem, recv_sem):
        copy = pltpu.make_async_remote_copy(
            src_ref=src, dst_ref=dst, send_sem=send_sem.at[k], recv_sem=recv_sem.at[opposite[k]],
            device_id=peers[k], device_id_type=MESH,
        )
        copy.start()
        return copy

    pl.semaphore_wait(barrier, 5)
    vel3 = vel_hbm.reshape(3, 64, 128)
    sends = [
        remote(vel3.at[:, pl.ds(0, 48), :], hx.at[1], 0, send_a, recv_a),
        remote(vel3.at[:, pl.ds(16, 48), :], hx.at[0], 1, send_a, recv_a),
    ]
    loads[0].wait()
    near = 13 * (1 - gy)
    for r in range(3):
        row = v[pl.ds(near + r, 16, stride=16), :]
        ysend[r] = row
        ydiag[r] = row.astype(BF16)
    sends += [
        remote(ysend, hy, 2, send_a, recv_a),
        remote(ydiag, hd.at[1], 3, send_a, recv_a),
        remote(ydiag, hd.at[0], 4, send_a, recv_a),
    ]

    @pl.loop(0, 10)
    def _(i):
        uf[pl.ds(i * URO, URO), :] = jnp.zeros((URO, 128), F32)

    def patch(field, x, c):
        for dz in range(3):
            start = x * URO + (2 * gy + 1) * 16 + dz * 3 + c
            uf[pl.ds(start, 16, stride=16), :] = spin(field, 1 - dz)

    def rounded(x):
        u16[pl.ds(x * URO, URO), :] = uf[pl.ds(x * URO, URO), :].astype(BF16)

    for c in range(3):
        for x in range(4):
            patch(v[pl.ds((c * 4 + x) * 16, 16), :], x + 3, c)
    for x in range(3, 7):
        rounded(x)

    loads[1].wait()
    wt0[...] = jnp.zeros_like(wt0)
    wt1[...] = jnp.zeros_like(wt1)
    for c in range(3):
        for dx in range(3):
            for dy in range(3):
                w = wi_raw[c, dx, dy].astype(F32)
                wide = jnp.concatenate([w, jnp.zeros_like(w)], axis=1)
                row = dx * 48 + dy * 16 + c
                wt0[pl.ds(row, 3, stride=3), :] = wide
                wt1[pl.ds(row + 48, 3, stride=3), :] = spin(wide, 64)
    wi[...] = (wt0[...] + wt1[...]).T[:, :192].astype(BF16)

    loads[2].wait()
    for dy in range(3):
        for dz in range(3):
            a, b, c, d = band(wm_raw[0, dy, dz], wm_raw[1, dy, dz], wm_raw[2, dy, dz])
            wp[pl.ds(dz * 128, 64), pl.ds(dy * 256, 128)] = a
            wp[pl.ds(dz * 128, 64), pl.ds(dy * 256 + 128, 128)] = b
            wp[pl.ds(dz * 128 + 64, 64), pl.ds(dy * 256, 128)] = c
            wp[pl.ds(dz * 128 + 64, 64), pl.ds(dy * 256 + 128, 128)] = d

    loads[3].wait()
    wof[...] = jnp.zeros_like(wof)
    for k in range(6):
        for dy in range(3):
            a, b, c, d = band(*(wo_raw[ORDER[k], dx, dy].astype(F32) for dx in range(3)))
            for x in range(4):
                first, second = ((a, b), (c, d))[x % 2]
                rows = pl.ds(dy * 72 + k * 4 + x, 3, stride=24)
                wof[x // 2, rows, :] = first
                wof[x // 2 + 1, rows, :] = second
    for m in range(3):
        wo[:, pl.ds(m * 128, 128)] = wof[m].astype(BF16)

    h1[0] = jnp.zeros((512, 128), BF16)
    h1[19] = jnp.zeros((512, 128), BF16)
    for dy in range(3):
        q[dy, 0] = jnp.zeros((24, 128), F32)
        q[dy, 19] = jnp.zeros((24, 128), F32)

    for k in range(2):
        sends[k].wait_recv()
    for side, x_to in ((0, 0), (1, 7)):
        for x in range(3):
            for c in range(3):
                patch(hx[side, c, pl.ds(x * 16, 16), :], x + x_to, c)
    for x in (0, 1, 2, 7, 8, 9):
        rounded(x)

    def place(i):
        return jnp.where(gy == 0, i, 8 - i) * 2

    def layer1(i):
        j = place(i)
        for p in range(4):
            def rows(dj):
                return jnp.concatenate(
                    [u16[pl.ds((2 * p + k) * URO + (j + dj) * 16, 48), :] for k in range(4)], axis=0
                )
            out = gelu(jnp.dot(wi[...], jnp.concatenate([rows(0), rows(1)], axis=1), preferred_element_type=F32))
            out = out.astype(BF16)
            h1[j + 1, pl.ds(p * 128, 128), :] = out[:, :128]
            h1[j + 2, pl.ds(p * 128, 128), :] = out[:, 128:]

    def layer2(i):
        j = place(i)
        for p in range(3):
            def rows(dj):
                return jnp.concatenate(
                    [h1[j + dj + dy, pl.ds(p * 128, 256), :] for dy in range(3)], axis=0
                )
            part = jnp.dot(wp[...], jnp.concatenate([rows(0), rows(1)], axis=1), preferred_element_type=F32)
            for dj in range(2):
                half = part[:, dj * 128:dj * 128 + 128]
                out = gelu(spin(half[0:128], 1) + half[128:256] + spin(half[256:384], -1))
                h2[j + dj, pl.ds(p * 128, 128), :] = out.astype(BF16)

    def layer3(i):
        j = place(i)
        part = jnp.dot(wo[...], jnp.concatenate([h2[j], h2[j + 1]], axis=1), preferred_element_type=F32)
        for dj in range(2):
            half = part[:, dj * 128:dj * 128 + 128]
            for dy in range(3):
                at = dy * 72
                q[dy, j + dj + 1] = (
                    spin(half[at:at + 24], 1) + half[at + 24:at + 48] + spin(half[at + 48:at + 72], -1)
                )

    def gather(i):
        j = place(i)
        for dj in range(2):
            total = q[0, j + dj] + q[1, j + dj + 1] + q[2, j + dj + 2]
            s[pl.ds(j + dj - 2 * gy, 24, stride=16), :] = total

    layer1(0)
    layer1(1)
    layer1(2)
    layer2(0)

    @pl.loop(3, 7)
    def _(i):
        layer3(i - 3)
        layer2(i - 2)
        layer1(i)

    for k in range(2, 5):
        sends[k].wait_recv()
    far = jnp.where(gy == 0, 17, 0)
    for r in range(3):
        for row, x_from, x_to, count in (
            (hy[r], 0, 3, 4), (hd[0, r].astype(F32), 1, 0, 3), (hd[1, r].astype(F32), 0, 7, 3)
        ):
            for dz in range(3):
                turned = spin(row, 1 - dz)
                for c in range(3):
                    start = x_to * URO + (far + r) * 16 + dz * 3 + c
                    uf[pl.ds(start, count, stride=URO), :] = turned[c * 4 + x_from:c * 4 + x_from + count]
    for x in range(10):
        at = x * URO + far * 16
        u16[pl.ds(at, 48), :] = uf[pl.ds(at, 48), :].astype(BF16)

    @pl.loop(7, 9)
    def _(i):
        layer3(i - 3)
        layer2(i - 2)
        layer1(i)
        gather(i - 7)

    layer3(6)
    layer2(7)
    gather(2)
    gather(3)
    layer3(7)
    layer2(8)
    gather(4)
    gather(5)
    layer3(8)
    gather(6)
    gather(7)

    for k in range(3):
        s16[k] = s[pl.ds(k * 64, 64), :].astype(BF16)
    last = [
        remote(s16.at[:, pl.ds(0, 48), :], sx.at[1], 0, send_b, recv_b),
        remote(s16.at[:, pl.ds(16, 48), :], sx.at[0], 1, send_b, recv_b),
    ]
    for r in range(3):
        ys16[r] = s[pl.ds(128 + near + r, 16, stride=16), :].astype(BF16)
    last.append(remote(ys16, sy, 2, send_b, recv_b))

    low_side = gy == 1

    def x_plane(c, x):
        if x < 0:
            return hx[0, c, pl.ds((x + 3) * 16, 16), :]
        if x > 3:
            return hx[1, c, pl.ds((x - 4) * 16, 16), :]
        return v[pl.ds((c * 4 + x) * 16, 16), :]

    def s_plane(k, x):
        if x < 0:
            return sx[0, k, pl.ds((x + 3) * 16, 16), :].astype(F32)
        if x > 3:
            return sx[1, k, pl.ds((x - 4) * 16, 16), :].astype(F32)
        return s[pl.ds((k * 4 + x) * 16, 16), :]

    for i in range(12):
        ve[pl.ds(i * 32 + 8, 16), :] = v[pl.ds(i * 16, 16), :]
        se[pl.ds(i * 32, 8), :] = jnp.zeros((8, 128), F32)
        se[pl.ds(i * 32 + 8, 16), :] = s[pl.ds(128 + i * 16, 16), :]
        se[pl.ds(i * 32 + 24, 8), :] = jnp.zeros((8, 128), F32)
    for r in range(3):
        row = hy[r, pl.ds(0, 12), :]
        ve[pl.ds(24 + r, 12, stride=32), :] = jnp.where(low_side, 0.0, row)
        ve[pl.ds(5 + r, 12, stride=32), :] = jnp.where(low_side, row, 0.0)
    parts = ((0, 0, 1), (2, 1, 4), (1, 2, 5))
    for c, (along_x, along_y, along_z) in enumerate(parts):
        for x in range(4):
            mid = x_plane(c, x)
            edge = s_plane(along_z, x)
            base = (c * 4 + x) * 32 + 8
            d1 = [0.0, 0.0, 0.0]
            d2 = (3.0 * CENTER) * mid
            div = 0.0
            for k in range(3):
                pairs = (
                    (x_plane(c, x + k + 1), x_plane(c, x - k - 1)),
                    (ve[pl.ds(base + k + 1, 16), :], ve[pl.ds(base - k - 1, 16), :]),
                    (spin(mid, -k - 1), spin(mid, k + 1)),
                )
                for a, (up, down) in enumerate(pairs):
                    d1[a] = d1[a] + A1[k] * (up - down)
                    d2 = d2 + A2[k] * (up + down)
                inner = (
                    (se[pl.ds(base + k + 1, 16), :] - se[pl.ds(base - k - 1, 16), :])
                    + (spin(edge, -k - 1) - spin(edge, k + 1))
                )
                if x + k + 1 < 4:
                    inner = inner + s_plane(along_x, x + k + 1)
                if x - k - 1 >= 0:
                    inner = inner - s_plane(along_x, x - k - 1)
                div = div + A1[k] * inner
            advect = x_plane(0, x) * d1[0] + x_plane(1, x) * d1[1] + x_plane(2, x) * d1[2]
            ten_ref[pl.ds((c * 4 + x) * 16, 16), :] = 0.2 * d2 - advect - div
    for k in range(6):
        str_ref[pl.ds(ORDER[k] * 64, 64), :] = s[pl.ds(k * 64, 64), :]

    last[2].wait_recv()
    rim = [sy[r].astype(F32)[:12] for r in range(3)]
    up = (
        A1[2] * rim[0],
        A1[1] * rim[0] + A1[2] * rim[1],
        A1[0] * rim[0] + A1[1] * rim[1] + A1[2] * rim[2],
    )
    down = (
        A1[0] * rim[2] + A1[1] * rim[1] + A1[2] * rim[0],
        A1[1] * rim[2] + A1[2] * rim[1],
        A1[2] * rim[2],
    )
    for r in range(3):
        at = pl.ds(near + r, 12, stride=16)
        ten_ref[at, :] = ten_ref[at, :] + jnp.where(low_side, down[r], -up[r])
    for k in range(2):
        last[k].wait_recv()
    for c, (along_x, _, _) in enumerate(parts):
        for x in range(4):
            at = pl.ds((c * 4 + x) * 16, 16)
            total = ten_ref[at, :]
            for k in range(3):
                if x + k + 1 > 3:
                    total = total - A1[k] * s_plane(along_x, x + k + 1)
                if x - k - 1 < 0:
                    total = total + A1[k] * s_plane(along_x, x - k - 1)
            ten_ref[at, :] = total

    for send in sends + last:
        send.wait_send()


def shards(velocity, kernel_in, kernel_mid, kernel_out):
    anywhere = pl.BlockSpec(memory_space=pltpu.HBM)
    whole = pl.BlockSpec(memory_space=pltpu.VMEM)
    tendency, stress = pl.pallas_call(
        kernel,
        out_shape=(pltpu.VMEM((192, 128), F32), pltpu.VMEM((384, 128), F32)),
        in_specs=[anywhere] * 4,
        out_specs=(whole, whole),
        scratch_shapes=[
            pltpu.VMEM((256, 128), F32),
            pltpu.VMEM((2, 3, 48, 128), F32),
            pltpu.VMEM((3, 16, 128), F32),
            pltpu.VMEM((2, 3, 16, 128), BF16),
            pltpu.VMEM((3, 16, 128), F32),
            pltpu.VMEM((3, 16, 128), BF16),
            pltpu.VMEM((10 * URO, 128), F32),
            pltpu.VMEM((10 * URO, 128), BF16),
            pltpu.VMEM((3, 3, 3, 3, 64), BF16),
            pltpu.VMEM((3, 3, 3, 64, 64), BF16),
            pltpu.VMEM((6, 3, 3, 3, 64), BF16),
            pltpu.VMEM((256, 128), F32),
            pltpu.VMEM((256, 128), F32),
            pltpu.VMEM((128, 192), BF16),
            pltpu.VMEM((384, 768), BF16),
            pltpu.VMEM((3, 216, 128), F32),
            pltpu.VMEM((216, 384), BF16),
            pltpu.VMEM((20, 512, 128), BF16),
            pltpu.VMEM((18, 384, 128), BF16),
            pltpu.VMEM((3, 20, 24, 128), F32),
            pltpu.VMEM((12 * 32, 128), F32),
            pltpu.VMEM((384, 128), F32),
            pltpu.VMEM((3, 64, 128), BF16),
            pltpu.VMEM((3, 16, 128), BF16),
            pltpu.VMEM((2, 3, 48, 128), BF16),
            pltpu.VMEM((3, 16, 128), BF16),
            pltpu.VMEM((12 * 32, 128), F32),
            pltpu.SemaphoreType.DMA((4,)),
            pltpu.SemaphoreType.DMA((5,)),
            pltpu.SemaphoreType.DMA((5,)),
            pltpu.SemaphoreType.DMA((3,)),
            pltpu.SemaphoreType.DMA((3,)),
        ],
        compiler_params=pltpu.CompilerParams(
            collective_id=0, has_side_effects=True, vmem_limit_bytes=60 * 1024 * 1024
        ),
    )(
        velocity.reshape(192, 128),
        jnp.transpose(kernel_in, (1, 2, 3, 4, 0)),
        jnp.transpose(kernel_mid, (2, 3, 4, 0, 1)),
        jnp.transpose(kernel_out, (0, 2, 3, 4, 1)),
    )
    return tendency.reshape(3, 4, 16, 128), stress.reshape(6, 4, 16, 128)


def solution(mesh):
    placed = (P(None, "gx", "gy", None), P(), P(), P())
    return jax.shard_map(
        shards,
        mesh=mesh,
        in_specs=placed,
        out_specs=(P(None, "gx", "gy", None), P(None, "gx", "gy", None)),
        check_vma=False,
    )
```

```python
import functools
import math

import jax
import jax.numpy as jnp
from jax import lax
from jax.experimental import pallas as pl
from jax.experimental.pallas import tpu as pltpu
from jax.sharding import PartitionSpec as P

MESH = pl.DeviceIdType.MESH
F32 = jnp.float32
BF16 = jnp.bfloat16

A1 = (0.75, -0.15, 1.0 / 60.0)
A2 = (1.5, -0.15, 1.0 / 90.0)
CENTER = -49.0 / 18.0
G0 = math.sqrt(2.0 / math.pi)
G1 = G0 * 0.044715

ORDER = (0, 4, 3, 1, 5, 2)
URO = 20 * 16


def gelu(s):
    half = 0.5 * s
    return half + half * jnp.tanh(s * (G0 + G1 * (s * s)))


def spin(a, k):
    return pltpu.roll(a, k % 128, 1)


def band(w0, w1, w2):
    zero = jnp.zeros_like(w0)
    cat = lambda a, b: jnp.concatenate([a, b], axis=1)
    return cat(w0, w1), cat(w2, zero), cat(zero, w0), cat(w1, w2)


def kernel(
    vel_hbm, wi_hbm, wm_hbm, wo_hbm, ten_ref, str_ref,
    v, hx, hy, hd, ysend, ydiag, uf, u16, wi_raw, wm_raw, wo_raw, wt0, wt1, wi, wp, wof, wo, h1, h2, q, ve, s, s16, ys16, sx, sy, se,
    load_sem, send_a, recv_a, send_b, recv_b,
):
    n = 128
    gx = lax.axis_index("gx")
    gy = lax.axis_index("gy")
    lo = lax.rem(gx + n - 1, n)
    hi = lax.rem(gx + 1, n)
    oy = 1 - gy
    peers = ((lo, gy), (hi, gy), (gx, oy), (lo, oy), (hi, oy))
    opposite = (1, 0, 2, 4, 3)

    barrier = pltpu.get_barrier_semaphore()
    for peer in peers:
        pl.semaphore_signal(barrier, inc=1, device_id=peer, device_id_type=MESH)
    loads = [
        pltpu.make_async_copy(vel_hbm, v.at[pl.ds(0, 192)], load_sem.at[0]),
        pltpu.make_async_copy(wi_hbm, wi_raw, load_sem.at[1]),
        pltpu.make_async_copy(wm_hbm, wm_raw, load_sem.at[2]),
        pltpu.make_async_copy(wo_hbm, wo_raw, load_sem.at[3]),
    ]
    for load in loads:
        load.start()
    v[pl.ds(192, 64), :] = jnp.zeros((64, 128), F32)

    def remote(src, dst, k, send_sem, recv_sem):
        copy = pltpu.make_async_remote_copy(
            src_ref=src, dst_ref=dst, send_sem=send_sem.at[k], recv_sem=recv_sem.at[opposite[k]],
            device_id=peers[k], device_id_type=MESH,
        )
        copy.start()
        return copy

    pl.semaphore_wait(barrier, 5)
    vel3 = vel_hbm.reshape(3, 64, 128)
    sends = [
        remote(vel3.at[:, pl.ds(0, 48), :], hx.at[1], 0, send_a, recv_a),
        remote(vel3.at[:, pl.ds(16, 48), :], hx.at[0], 1, send_a, recv_a),
    ]
    loads[0].wait()
    near = 13 * (1 - gy)
    for r in range(3):
        row = v[pl.ds(near + r, 16, stride=16), :]
        ysend[r] = row
        ydiag[r] = row.astype(BF16)
    sends += [
        remote(ysend, hy, 2, send_a, recv_a),
        remote(ydiag, hd.at[1], 3, send_a, recv_a),
        remote(ydiag, hd.at[0], 4, send_a, recv_a),
    ]

    @pl.loop(0, 10)
    def _(i):
        uf[pl.ds(i * URO, URO), :] = jnp.zeros((URO, 128), F32)

    def patch(field, x, c):
        for dz in range(3):
            start = x * URO + (2 * gy + 1) * 16 + dz * 3 + c
            uf[pl.ds(start, 16, stride=16), :] = spin(field, 1 - dz)

    def rounded(x):
        u16[pl.ds(x * URO, URO), :] = uf[pl.ds(x * URO, URO), :].astype(BF16)

    for c in range(3):
        for x in range(4):
            patch(v[pl.ds((c * 4 + x) * 16, 16), :], x + 3, c)
    for x in range(3, 7):
        rounded(x)

    def outward(dy):
        return jnp.where(gy == 0, dy, 2 - dy)

    loads[1].wait()
    wt0[...] = jnp.zeros_like(wt0)
    wt1[...] = jnp.zeros_like(wt1)
    for c in range(3):
        for dx in range(3):
            for dy in range(3):
                w = wi_raw[c, dx, dy].astype(F32)
                wide = jnp.concatenate([w, jnp.zeros_like(w)], axis=1)
                row = dx * 48 + dy * 16 + c
                wt0[pl.ds(row, 3, stride=3), :] = wide
                wt1[pl.ds(row + 48, 3, stride=3), :] = spin(wide, 64)
    wi[...] = (wt0[...] + wt1[...]).T[:, :192].astype(BF16)

    loads[2].wait()
    for dy in range(3):
        for dz in range(3):
            a, b, c, d = band(*(wm_raw[dx, outward(dy), dz] for dx in range(3)))
            wp[pl.ds(dz * 128, 64), pl.ds(dy * 256, 128)] = a
            wp[pl.ds(dz * 128, 64), pl.ds(dy * 256 + 128, 128)] = b
            wp[pl.ds(dz * 128 + 64, 64), pl.ds(dy * 256, 128)] = c
            wp[pl.ds(dz * 128 + 64, 64), pl.ds(dy * 256 + 128, 128)] = d

    loads[3].wait()
    wof[...] = jnp.zeros_like(wof)
    for k in range(6):
        for dy in range(3):
            a, b, c, d = band(*(wo_raw[ORDER[k], dx, outward(dy)].astype(F32) for dx in range(3)))
            for x in range(4):
                first, second = ((a, b), (c, d))[x % 2]
                rows = pl.ds(dy * 72 + k * 4 + x, 3, stride=24)
                wof[x // 2, rows, :] = first
                wof[x // 2 + 1, rows, :] = second
    for m in range(3):
        wo[:, pl.ds(m * 128, 128)] = wof[m].astype(BF16)

    h1[0] = jnp.zeros((512, 128), BF16)
    h1[19] = jnp.zeros((512, 128), BF16)
    for dy in range(3):
        q[dy, 0] = jnp.zeros((24, 128), F32)
        q[dy, 19] = jnp.zeros((24, 128), F32)

    for k in range(2):
        sends[k].wait_recv()
    for side, x_to in ((0, 0), (1, 7)):
        for x in range(3):
            for c in range(3):
                patch(hx[side, c, pl.ds(x * 16, 16), :], x + x_to, c)
    for x in (0, 1, 2, 7, 8, 9):
        rounded(x)

    def layer1(i, p):
        def rows(e):
            j = jnp.where(gy == 0, 2 * i + e, 17 - 2 * i - e)
            return jnp.concatenate(
                [u16[pl.ds((2 * p + k) * URO + j * 16, 48), :] for k in range(4)], axis=0
            )
        out = gelu(jnp.dot(wi[...], jnp.concatenate([rows(0), rows(1)], axis=1), preferred_element_type=F32))
        out = out.astype(BF16)
        h1[2 * i + 1, pl.ds(p * 128, 128), :] = out[:, :128]
        h1[2 * i + 2, pl.ds(p * 128, 128), :] = out[:, 128:]

    def layer2(i, p):
        def rows(e):
            return jnp.concatenate(
                [h1[2 * i + e + dy, pl.ds(p * 128, 256), :] for dy in range(3)], axis=0
            )
        part = jnp.dot(wp[...], jnp.concatenate([rows(0), rows(1)], axis=1), preferred_element_type=F32)
        for e in range(2):
            half = part[:, e * 128:e * 128 + 128]
            out = gelu(spin(half[0:128], 1) + half[128:256] + spin(half[256:384], -1))
            h2[2 * i + e, pl.ds(p * 128, 128), :] = out.astype(BF16)

    def layer3(i):
        part = jnp.dot(wo[...], jnp.concatenate([h2[2 * i], h2[2 * i + 1]], axis=1), preferred_element_type=F32)
        for e in range(2):
            half = part[:, e * 128:e * 128 + 128]
            for dy in range(3):
                at = dy * 72
                q[dy, 2 * i + e + 1] = (
                    spin(half[at:at + 24], 1) + half[at + 24:at + 48] + spin(half[at + 48:at + 72], -1)
                )

    def gather(i):
        for e in range(2):
            d = 2 * i + e
            total = q[0, d] + q[1, d + 1] + q[2, d + 2]
            s[pl.ds(jnp.where(gy == 0, d, 15 - d), 24, stride=16), :] = total

    def step(first, second, third, gathered=()):
        for p in range(4):
            if second is not None and p < 3:
                layer2(second, p)
            if first is not None:
                layer1(first, p)
            if third is not None and p == 2:
                layer3(third)
        for i in gathered:
            gather(i)
    step(0, None, None)
    step(1, None, None)
    step(2, 0, None)

    @pl.loop(3, 7)
    def _(i):
        step(i, i - 2, i - 3)

    for k in range(2, 5):
        sends[k].wait_recv()
    far = jnp.where(gy == 0, 17, 0)
    for r in range(3):
        for row, x_from, x_to, count in (
            (hy[r], 0, 3, 4), (hd[0, r].astype(F32), 1, 0, 3), (hd[1, r].astype(F32), 0, 7, 3)
        ):
            for dz in range(3):
                turned = spin(row, 1 - dz)
                for c in range(3):
                    start = x_to * URO + (far + r) * 16 + dz * 3 + c
                    uf[pl.ds(start, count, stride=URO), :] = turned[c * 4 + x_from:c * 4 + x_from + count]
    for x in range(10):
        at = x * URO + far * 16
        u16[pl.ds(at, 48), :] = uf[pl.ds(at, 48), :].astype(BF16)

    @pl.loop(7, 9)
    def _(i):
        step(i, i - 2, i - 3, (i - 7,))

    step(None, 7, 6, (2, 3))
    step(None, 8, 7, (4, 5))
    step(None, None, 8, (6, 7))

    for k in range(3):
        s16[k] = s[pl.ds(k * 64, 64), :].astype(BF16)
    last = [
        remote(s16.at[:, pl.ds(0, 48), :], sx.at[1], 0, send_b, recv_b),
        remote(s16.at[:, pl.ds(16, 48), :], sx.at[0], 1, send_b, recv_b),
    ]
    for r in range(3):
        ys16[r] = s[pl.ds(128 + near + r, 16, stride=16), :].astype(BF16)
    last.append(remote(ys16, sy, 2, send_b, recv_b))

    low_side = gy == 1

    def x_plane(c, x):
        if x < 0:
            return hx[0, c, pl.ds((x + 3) * 16, 16), :]
        if x > 3:
            return hx[1, c, pl.ds((x - 4) * 16, 16), :]
        return v[pl.ds((c * 4 + x) * 16, 16), :]

    def s_plane(k, x):
        if x < 0:
            return sx[0, k, pl.ds((x + 3) * 16, 16), :].astype(F32)
        if x > 3:
            return sx[1, k, pl.ds((x - 4) * 16, 16), :].astype(F32)
        return s[pl.ds((k * 4 + x) * 16, 16), :]

    for i in range(12):
        ve[pl.ds(i * 32 + 8, 16), :] = v[pl.ds(i * 16, 16), :]
        se[pl.ds(i * 32, 8), :] = jnp.zeros((8, 128), F32)
        se[pl.ds(i * 32 + 8, 16), :] = s[pl.ds(128 + i * 16, 16), :]
        se[pl.ds(i * 32 + 24, 8), :] = jnp.zeros((8, 128), F32)
    for r in range(3):
        row = hy[r, pl.ds(0, 12), :]
        ve[pl.ds(24 + r, 12, stride=32), :] = jnp.where(low_side, 0.0, row)
        ve[pl.ds(5 + r, 12, stride=32), :] = jnp.where(low_side, row, 0.0)
    parts = ((0, 0, 1), (2, 1, 4), (1, 2, 5))
    for c, (along_x, along_y, along_z) in enumerate(parts):
        for x in range(4):
            mid = x_plane(c, x)
            edge = s_plane(along_z, x)
            base = (c * 4 + x) * 32 + 8
            d1 = [0.0, 0.0, 0.0]
            d2 = (3.0 * CENTER) * mid
            div = 0.0
            for k in range(3):
                pairs = (
                    (x_plane(c, x + k + 1), x_plane(c, x - k - 1)),
                    (ve[pl.ds(base + k + 1, 16), :], ve[pl.ds(base - k - 1, 16), :]),
                    (spin(mid, -k - 1), spin(mid, k + 1)),
                )
                for a, (up, down) in enumerate(pairs):
                    d1[a] = d1[a] + A1[k] * (up - down)
                    d2 = d2 + A2[k] * (up + down)
                inner = (
                    (se[pl.ds(base + k + 1, 16), :] - se[pl.ds(base - k - 1, 16), :])
                    + (spin(edge, -k - 1) - spin(edge, k + 1))
                )
                if x + k + 1 < 4:
                    inner = inner + s_plane(along_x, x + k + 1)
                if x - k - 1 >= 0:
                    inner = inner - s_plane(along_x, x - k - 1)
                div = div + A1[k] * inner
            advect = x_plane(0, x) * d1[0] + x_plane(1, x) * d1[1] + x_plane(2, x) * d1[2]
            ten_ref[pl.ds((c * 4 + x) * 16, 16), :] = 0.2 * d2 - advect - div
    for k in range(6):
        str_ref[pl.ds(ORDER[k] * 64, 64), :] = s[pl.ds(k * 64, 64), :]

    last[2].wait_recv()
    rim = [sy[r].astype(F32)[:12] for r in range(3)]
    up = (
        A1[2] * rim[0],
        A1[1] * rim[0] + A1[2] * rim[1],
        A1[0] * rim[0] + A1[1] * rim[1] + A1[2] * rim[2],
    )
    down = (
        A1[0] * rim[2] + A1[1] * rim[1] + A1[2] * rim[0],
        A1[1] * rim[2] + A1[2] * rim[1],
        A1[2] * rim[2],
    )
    for r in range(3):
        at = pl.ds(near + r, 12, stride=16)
        ten_ref[at, :] = ten_ref[at, :] + jnp.where(low_side, down[r], -up[r])
    for k in range(2):
        last[k].wait_recv()
    for c, (along_x, _, _) in enumerate(parts):
        for x in range(4):
            at = pl.ds((c * 4 + x) * 16, 16)
            total = ten_ref[at, :]
            for k in range(3):
                if x + k + 1 > 3:
                    total = total - A1[k] * s_plane(along_x, x + k + 1)
                if x - k - 1 < 0:
                    total = total + A1[k] * s_plane(along_x, x - k - 1)
            ten_ref[at, :] = total

    for send in sends + last:
        send.wait_send()


def emit(ten_vmem, str_vmem, ten_hbm, str_hbm, sem):
    copies = [
        pltpu.make_async_copy(str_vmem, str_hbm, sem.at[0]),
        pltpu.make_async_copy(ten_vmem, ten_hbm, sem.at[1]),
    ]
    for copy in copies:
        copy.start()
    for copy in copies:
        copy.wait()


def shards(velocity, kernel_in, kernel_mid, kernel_out):
    anywhere = pl.BlockSpec(memory_space=pltpu.HBM)
    whole = pl.BlockSpec(memory_space=pltpu.VMEM)
    tendency, stress = pl.pallas_call(
        kernel,
        out_shape=(pltpu.VMEM((192, 128), F32), pltpu.VMEM((384, 128), F32)),
        in_specs=[anywhere] * 4,
        out_specs=(whole, whole),
        scratch_shapes=[
            pltpu.VMEM((256, 128), F32),
            pltpu.VMEM((2, 3, 48, 128), F32),
            pltpu.VMEM((3, 16, 128), F32),
            pltpu.VMEM((2, 3, 16, 128), BF16),
            pltpu.VMEM((3, 16, 128), F32),
            pltpu.VMEM((3, 16, 128), BF16),
            pltpu.VMEM((10 * URO, 128), F32),
            pltpu.VMEM((10 * URO, 128), BF16),
            pltpu.VMEM((3, 3, 3, 3, 64), BF16),
            pltpu.VMEM((3, 3, 3, 64, 64), BF16),
            pltpu.VMEM((6, 3, 3, 3, 64), BF16),
            pltpu.VMEM((256, 128), F32),
            pltpu.VMEM((256, 128), F32),
            pltpu.VMEM((128, 192), BF16),
            pltpu.VMEM((384, 768), BF16),
            pltpu.VMEM((3, 216, 128), F32),
            pltpu.VMEM((216, 384), BF16),
            pltpu.VMEM((20, 512, 128), BF16),
            pltpu.VMEM((18, 384, 128), BF16),
            pltpu.VMEM((3, 20, 24, 128), F32),
            pltpu.VMEM((12 * 32, 128), F32),
            pltpu.VMEM((384, 128), F32),
            pltpu.VMEM((3, 64, 128), BF16),
            pltpu.VMEM((3, 16, 128), BF16),
            pltpu.VMEM((2, 3, 48, 128), BF16),
            pltpu.VMEM((3, 16, 128), BF16),
            pltpu.VMEM((12 * 32, 128), F32),
            pltpu.SemaphoreType.DMA((4,)),
            pltpu.SemaphoreType.DMA((5,)),
            pltpu.SemaphoreType.DMA((5,)),
            pltpu.SemaphoreType.DMA((3,)),
            pltpu.SemaphoreType.DMA((3,)),
        ],
        compiler_params=pltpu.CompilerParams(
            collective_id=0, has_side_effects=True, vmem_limit_bytes=60 * 1024 * 1024
        ),
    )(
        velocity.reshape(192, 128),
        jnp.transpose(kernel_in, (1, 2, 3, 4, 0)),
        jnp.transpose(kernel_mid, (2, 3, 4, 0, 1)),
        jnp.transpose(kernel_out, (0, 2, 3, 4, 1)),
    )
    free = pl.BlockSpec(memory_space=pl.ANY)
    tendency, stress = pl.pallas_call(
        emit,
        out_shape=(jax.ShapeDtypeStruct((192, 128), F32), jax.ShapeDtypeStruct((384, 128), F32)),
        in_specs=(free, free),
        out_specs=(free, free),
        scratch_shapes=[pltpu.SemaphoreType.DMA((2,))],
        compiler_params=pltpu.CompilerParams(vmem_limit_bytes=1024 * 1024),
    )(tendency, stress)
    return tendency.reshape(3, 4, 16, 128), stress.reshape(6, 4, 16, 128)


def solution(mesh):
    placed = (P(None, "gx", "gy", None), P(), P(), P())
    return jax.shard_map(
        shards,
        mesh=mesh,
        in_specs=placed,
        out_specs=(P(None, "gx", "gy", None), P(None, "gx", "gy", None)),
        check_vma=False,
    )
```

```python
import functools
import math

import jax
import jax.numpy as jnp
from jax import lax
from jax.experimental import pallas as pl
from jax.experimental.pallas import tpu as pltpu
from jax.sharding import PartitionSpec as P

MESH = pl.DeviceIdType.MESH
F32 = jnp.float32
BF16 = jnp.bfloat16

A1 = (0.75, -0.15, 1.0 / 60.0)
A2 = (1.5, -0.15, 1.0 / 90.0)
CENTER = -49.0 / 18.0
G0 = math.sqrt(2.0 / math.pi)
G1 = G0 * 0.044715

ORDER = (0, 4, 3, 1, 5, 2)
URO = 20 * 16


def gelu(s):
    half = 0.5 * s
    return half + half * jnp.tanh(s * (G0 + G1 * (s * s)))


def spin(a, k):
    return pltpu.roll(a, k % 128, 1)


def band(w0, w1, w2):
    zero = jnp.zeros_like(w0)
    cat = lambda a, b: jnp.concatenate([a, b], axis=1)
    return cat(w0, w1), cat(w2, zero), cat(zero, w0), cat(w1, w2)


def kernel(
    vel_hbm, wi_hbm, wm_hbm, wo_hbm, ten_ref, str_ref,
    v, hx, hy, hd, ysend, ydiag, uf, u16, wi_raw, wm_raw, wo_raw, wt0, wt1, wi, wp, wof, wo, h1, h2, q, ve, s, s16, ys16, sx, sy, se,
    load_sem, send_a, recv_a, send_b, recv_b,
):
    n = 128
    gx = lax.axis_index("gx")
    gy = lax.axis_index("gy")
    lo = lax.rem(gx + n - 1, n)
    hi = lax.rem(gx + 1, n)
    oy = 1 - gy
    peers = ((lo, gy), (hi, gy), (gx, oy), (lo, oy), (hi, oy))
    opposite = (1, 0, 2, 4, 3)

    barrier = pltpu.get_barrier_semaphore()
    for peer in peers:
        pl.semaphore_signal(barrier, inc=1, device_id=peer, device_id_type=MESH)
    loads = [
        pltpu.make_async_copy(vel_hbm, v.at[pl.ds(0, 192)], load_sem.at[0]),
        pltpu.make_async_copy(wi_hbm, wi_raw, load_sem.at[1]),
        pltpu.make_async_copy(wm_hbm, wm_raw, load_sem.at[2]),
        pltpu.make_async_copy(wo_hbm, wo_raw, load_sem.at[3]),
    ]
    for load in loads:
        load.start()
    v[pl.ds(192, 64), :] = jnp.zeros((64, 128), F32)

    def remote(src, dst, k, send_sem, recv_sem):
        copy = pltpu.make_async_remote_copy(
            src_ref=src, dst_ref=dst, send_sem=send_sem.at[k], recv_sem=recv_sem.at[opposite[k]],
            device_id=peers[k], device_id_type=MESH,
        )
        copy.start()
        return copy

    pl.semaphore_wait(barrier, 5)
    vel3 = vel_hbm.reshape(3, 64, 128)
    sends = [
        remote(vel3.at[:, pl.ds(0, 48), :], hx.at[1], 0, send_a, recv_a),
        remote(vel3.at[:, pl.ds(16, 48), :], hx.at[0], 1, send_a, recv_a),
    ]
    loads[0].wait()
    near = 13 * (1 - gy)
    for r in range(3):
        row = v[pl.ds(near + r, 16, stride=16), :]
        ysend[r] = row
        ydiag[r] = row.astype(BF16)
    sends += [
        remote(ysend, hy, 2, send_a, recv_a),
        remote(ydiag, hd.at[1], 3, send_a, recv_a),
        remote(ydiag, hd.at[0], 4, send_a, recv_a),
    ]

    @pl.loop(0, 10)
    def _(i):
        uf[pl.ds(i * URO, URO), :] = jnp.zeros((URO, 128), F32)

    def patch(field, x, c):
        for dz in range(3):
            start = x * URO + (2 * gy + 1) * 16 + dz * 3 + c
            uf[pl.ds(start, 16, stride=16), :] = spin(field, 1 - dz)

    def rounded(x):
        u16[pl.ds(x * URO, URO), :] = uf[pl.ds(x * URO, URO), :].astype(BF16)

    for c in range(3):
        for x in range(4):
            patch(v[pl.ds((c * 4 + x) * 16, 16), :], x + 3, c)
    for x in range(3, 7):
        rounded(x)

    def outward(dy):
        return jnp.where(gy == 0, dy, 2 - dy)

    loads[1].wait()
    wt0[...] = jnp.zeros_like(wt0)
    wt1[...] = jnp.zeros_like(wt1)
    for c in range(3):
        for dx in range(3):
            for dy in range(3):
                w = wi_raw[c, dx, dy].astype(F32)
                wide = jnp.concatenate([w, jnp.zeros_like(w)], axis=1)
                row = dx * 48 + dy * 16 + c
                wt0[pl.ds(row, 3, stride=3), :] = wide
                wt1[pl.ds(row + 48, 3, stride=3), :] = spin(wide, 64)
    wi[...] = (wt0[...] + wt1[...]).T[:, :192].astype(BF16)

    loads[2].wait()
    for dy in range(3):
        for dz in range(3):
            a, b, c, d = band(*(wm_raw[dx, outward(dy), dz] for dx in range(3)))
            wp[pl.ds(dz * 128, 64), pl.ds(dy * 256, 128)] = a
            wp[pl.ds(dz * 128, 64), pl.ds(dy * 256 + 128, 128)] = b
            wp[pl.ds(dz * 128 + 64, 64), pl.ds(dy * 256, 128)] = c
            wp[pl.ds(dz * 128 + 64, 64), pl.ds(dy * 256 + 128, 128)] = d

    loads[3].wait()
    wof[...] = jnp.zeros_like(wof)
    for k in range(6):
        for dy in range(3):
            a, b, c, d = band(*(wo_raw[ORDER[k], dx, outward(dy)].astype(F32) for dx in range(3)))
            for x in range(4):
                first, second = ((a, b), (c, d))[x % 2]
                rows = pl.ds(dy * 72 + k * 4 + x, 3, stride=24)
                wof[x // 2, rows, :] = first
                wof[x // 2 + 1, rows, :] = second
    for m in range(3):
        wo[:, pl.ds(m * 128, 128)] = wof[m].astype(BF16)

    h1[0] = jnp.zeros((512, 128), BF16)
    h1[19] = jnp.zeros((512, 128), BF16)
    for dy in range(3):
        q[dy, 0] = jnp.zeros((24, 128), F32)
        q[dy, 19] = jnp.zeros((24, 128), F32)

    for k in range(2):
        sends[k].wait_recv()
    for side, x_to in ((0, 0), (1, 7)):
        for x in range(3):
            for c in range(3):
                patch(hx[side, c, pl.ds(x * 16, 16), :], x + x_to, c)
    for x in (0, 1, 2, 7, 8, 9):
        rounded(x)

    def layer1(i, p):
        def rows(e):
            j = jnp.where(gy == 0, 2 * i + e, 17 - 2 * i - e)
            return jnp.concatenate(
                [u16[pl.ds((2 * p + k) * URO + j * 16, 48), :] for k in range(4)], axis=0
            )
        out = gelu(jnp.dot(wi[...], jnp.concatenate([rows(0), rows(1)], axis=1), preferred_element_type=F32))
        out = out.astype(BF16)
        h1[2 * i + 1, pl.ds(p * 128, 128), :] = out[:, :128]
        h1[2 * i + 2, pl.ds(p * 128, 128), :] = out[:, 128:]

    def layer2(i, p):
        def rows(e):
            return jnp.concatenate(
                [h1[2 * i + e + dy, pl.ds(p * 128, 256), :] for dy in range(3)], axis=0
            )
        part = jnp.dot(wp[...], jnp.concatenate([rows(0), rows(1)], axis=1), preferred_element_type=F32)
        for e in range(2):
            half = part[:, e * 128:e * 128 + 128]
            out = gelu(spin(half[0:128], 1) + half[128:256] + spin(half[256:384], -1))
            h2[2 * i + e, pl.ds(p * 128, 128), :] = out.astype(BF16)

    def layer2_last():
        for places in ((0, 1), (2,)):
            rhs = [
                jnp.concatenate([h1[16 + dy, pl.ds(p * 128, 256), :] for dy in range(3)], axis=0) for p in places
            ]
            rhs = jnp.concatenate(rhs, axis=1) if len(places) > 1 else rhs[0]
            part = jnp.dot(wp[...], rhs, preferred_element_type=F32)
            for k, p in enumerate(places):
                half = part[:, k * 128:k * 128 + 128]
                out = gelu(spin(half[0:128], 1) + half[128:256] + spin(half[256:384], -1))
                h2[16, pl.ds(p * 128, 128), :] = out.astype(BF16)

    def layer3_last():
        half = jnp.dot(wo[...], h2[16], preferred_element_type=F32)
        for dy in range(3):
            at = dy * 72
            q[dy, 17] = spin(half[at:at + 24], 1) + half[at + 24:at + 48] + spin(half[at + 48:at + 72], -1)

    def layer3(i):
        part = jnp.dot(wo[...], jnp.concatenate([h2[2 * i], h2[2 * i + 1]], axis=1), preferred_element_type=F32)
        for e in range(2):
            half = part[:, e * 128:e * 128 + 128]
            for dy in range(3):
                at = dy * 72
                q[dy, 2 * i + e + 1] = (
                    spin(half[at:at + 24], 1) + half[at + 24:at + 48] + spin(half[at + 48:at + 72], -1)
                )

    def gather(i):
        for e in range(2):
            d = 2 * i + e
            total = q[0, d] + q[1, d + 1] + q[2, d + 2]
            s[pl.ds(jnp.where(gy == 0, d, 15 - d), 24, stride=16), :] = total

    def step(first, second, third, gathered=()):
        for p in range(4):
            if second is not None and p < 3:
                layer2(second, p)
            if first is not None:
                layer1(first, p)
            if third is not None and p == 2:
                layer3(third)
        for i in gathered:
            gather(i)
    step(0, None, None)
    step(1, None, None)
    step(2, 0, None)

    for i in range(3, 7):
        step(i, i - 2, i - 3)

    for k in range(2, 5):
        sends[k].wait_recv()
    far = jnp.where(gy == 0, 17, 0)
    for r in range(3):
        for row, x_from, x_to, count in (
            (hy[r], 0, 3, 4), (hd[0, r].astype(F32), 1, 0, 3), (hd[1, r].astype(F32), 0, 7, 3)
        ):
            for dz in range(3):
                turned = spin(row, 1 - dz)
                for c in range(3):
                    start = x_to * URO + (far + r) * 16 + dz * 3 + c
                    uf[pl.ds(start, count, stride=URO), :] = turned[c * 4 + x_from:c * 4 + x_from + count]
    for x in range(10):
        at = x * URO + far * 16
        u16[pl.ds(at, 48), :] = uf[pl.ds(at, 48), :].astype(BF16)

    for i in range(7, 9):
        step(i, i - 2, i - 3, (i - 7,))

    step(None, 7, 6, (2, 3))
    layer2_last()
    step(None, None, 7, (4, 5))
    layer3_last()
    gather(6)
    gather(7)

    for k in range(3):
        s16[k] = s[pl.ds(k * 64, 64), :].astype(BF16)
    last = [
        remote(s16.at[:, pl.ds(0, 48), :], sx.at[1], 0, send_b, recv_b),
        remote(s16.at[:, pl.ds(16, 48), :], sx.at[0], 1, send_b, recv_b),
    ]
    for r in range(3):
        ys16[r] = s[pl.ds(128 + near + r, 16, stride=16), :].astype(BF16)
    last.append(remote(ys16, sy, 2, send_b, recv_b))

    low_side = gy == 1

    def x_plane(c, x):
        if x < 0:
            return hx[0, c, pl.ds((x + 3) * 16, 16), :]
        if x > 3:
            return hx[1, c, pl.ds((x - 4) * 16, 16), :]
        return v[pl.ds((c * 4 + x) * 16, 16), :]

    def s_plane(k, x):
        if x < 0:
            return sx[0, k, pl.ds((x + 3) * 16, 16), :].astype(F32)
        if x > 3:
            return sx[1, k, pl.ds((x - 4) * 16, 16), :].astype(F32)
        return s[pl.ds((k * 4 + x) * 16, 16), :]

    for i in range(12):
        ve[pl.ds(i * 32 + 8, 16), :] = v[pl.ds(i * 16, 16), :]
        se[pl.ds(i * 32, 8), :] = jnp.zeros((8, 128), F32)
        se[pl.ds(i * 32 + 8, 16), :] = s[pl.ds(128 + i * 16, 16), :]
        se[pl.ds(i * 32 + 24, 8), :] = jnp.zeros((8, 128), F32)
    for r in range(3):
        row = hy[r, pl.ds(0, 12), :]
        ve[pl.ds(24 + r, 12, stride=32), :] = jnp.where(low_side, 0.0, row)
        ve[pl.ds(5 + r, 12, stride=32), :] = jnp.where(low_side, row, 0.0)
    parts = ((0, 0, 1), (2, 1, 4), (1, 2, 5))
    for c, (along_x, along_y, along_z) in enumerate(parts):
        for x in range(4):
            mid = x_plane(c, x)
            edge = s_plane(along_z, x)
            base = (c * 4 + x) * 32 + 8
            d1 = [0.0, 0.0, 0.0]
            d2 = (3.0 * CENTER) * mid
            div = 0.0
            for k in range(3):
                pairs = (
                    (x_plane(c, x + k + 1), x_plane(c, x - k - 1)),
                    (ve[pl.ds(base + k + 1, 16), :], ve[pl.ds(base - k - 1, 16), :]),
                    (spin(mid, -k - 1), spin(mid, k + 1)),
                )
                for a, (up, down) in enumerate(pairs):
                    d1[a] = d1[a] + A1[k] * (up - down)
                    d2 = d2 + A2[k] * (up + down)
                inner = (
                    (se[pl.ds(base + k + 1, 16), :] - se[pl.ds(base - k - 1, 16), :])
                    + (spin(edge, -k - 1) - spin(edge, k + 1))
                )
                if x + k + 1 < 4:
                    inner = inner + s_plane(along_x, x + k + 1)
                if x - k - 1 >= 0:
                    inner = inner - s_plane(along_x, x - k - 1)
                div = div + A1[k] * inner
            advect = x_plane(0, x) * d1[0] + x_plane(1, x) * d1[1] + x_plane(2, x) * d1[2]
            ten_ref[pl.ds((c * 4 + x) * 16, 16), :] = 0.2 * d2 - advect - div
    for k in range(6):
        str_ref[pl.ds(ORDER[k] * 64, 64), :] = s[pl.ds(k * 64, 64), :]

    last[2].wait_recv()
    rim = [sy[r].astype(F32)[:12] for r in range(3)]
    up = (
        A1[2] * rim[0],
        A1[1] * rim[0] + A1[2] * rim[1],
        A1[0] * rim[0] + A1[1] * rim[1] + A1[2] * rim[2],
    )
    down = (
        A1[0] * rim[2] + A1[1] * rim[1] + A1[2] * rim[0],
        A1[1] * rim[2] + A1[2] * rim[1],
        A1[2] * rim[2],
    )
    for r in range(3):
        at = pl.ds(near + r, 12, stride=16)
        ten_ref[at, :] = ten_ref[at, :] + jnp.where(low_side, down[r], -up[r])
    for k in range(2):
        last[k].wait_recv()
    for c, (along_x, _, _) in enumerate(parts):
        for x in range(4):
            at = pl.ds((c * 4 + x) * 16, 16)
            total = ten_ref[at, :]
            for k in range(3):
                if x + k + 1 > 3:
                    total = total - A1[k] * s_plane(along_x, x + k + 1)
                if x - k - 1 < 0:
                    total = total + A1[k] * s_plane(along_x, x - k - 1)
            ten_ref[at, :] = total

    for send in sends + last:
        send.wait_send()


def emit(ten_vmem, str_vmem, ten_hbm, str_hbm, sem):
    copies = [
        pltpu.make_async_copy(str_vmem, str_hbm, sem.at[0]),
        pltpu.make_async_copy(ten_vmem, ten_hbm, sem.at[1]),
    ]
    for copy in copies:
        copy.start()
    for copy in copies:
        copy.wait()


def shards(velocity, kernel_in, kernel_mid, kernel_out):
    anywhere = pl.BlockSpec(memory_space=pltpu.HBM)
    whole = pl.BlockSpec(memory_space=pltpu.VMEM)
    tendency, stress = pl.pallas_call(
        kernel,
        out_shape=(pltpu.VMEM((192, 128), F32), pltpu.VMEM((384, 128), F32)),
        in_specs=[anywhere] * 4,
        out_specs=(whole, whole),
        scratch_shapes=[
            pltpu.VMEM((256, 128), F32),
            pltpu.VMEM((2, 3, 48, 128), F32),
            pltpu.VMEM((3, 16, 128), F32),
            pltpu.VMEM((2, 3, 16, 128), BF16),
            pltpu.VMEM((3, 16, 128), F32),
            pltpu.VMEM((3, 16, 128), BF16),
            pltpu.VMEM((10 * URO, 128), F32),
            pltpu.VMEM((10 * URO, 128), BF16),
            pltpu.VMEM((3, 3, 3, 3, 64), BF16),
            pltpu.VMEM((3, 3, 3, 64, 64), BF16),
            pltpu.VMEM((6, 3, 3, 3, 64), BF16),
            pltpu.VMEM((256, 128), F32),
            pltpu.VMEM((256, 128), F32),
            pltpu.VMEM((128, 192), BF16),
            pltpu.VMEM((384, 768), BF16),
            pltpu.VMEM((3, 216, 128), F32),
            pltpu.VMEM((216, 384), BF16),
            pltpu.VMEM((20, 512, 128), BF16),
            pltpu.VMEM((17, 384, 128), BF16),
            pltpu.VMEM((3, 20, 24, 128), F32),
            pltpu.VMEM((12 * 32, 128), F32),
            pltpu.VMEM((384, 128), F32),
            pltpu.VMEM((3, 64, 128), BF16),
            pltpu.VMEM((3, 16, 128), BF16),
            pltpu.VMEM((2, 3, 48, 128), BF16),
            pltpu.VMEM((3, 16, 128), BF16),
            pltpu.VMEM((12 * 32, 128), F32),
            pltpu.SemaphoreType.DMA((4,)),
            pltpu.SemaphoreType.DMA((5,)),
            pltpu.SemaphoreType.DMA((5,)),
            pltpu.SemaphoreType.DMA((3,)),
            pltpu.SemaphoreType.DMA((3,)),
        ],
        compiler_params=pltpu.CompilerParams(
            collective_id=0, has_side_effects=True, vmem_limit_bytes=60 * 1024 * 1024
        ),
    )(
        velocity.reshape(192, 128),
        jnp.transpose(kernel_in, (1, 2, 3, 4, 0)),
        jnp.transpose(kernel_mid, (2, 3, 4, 0, 1)),
        jnp.transpose(kernel_out, (0, 2, 3, 4, 1)),
    )
    free = pl.BlockSpec(memory_space=pl.ANY)
    tendency, stress = pl.pallas_call(
        emit,
        out_shape=(jax.ShapeDtypeStruct((192, 128), F32), jax.ShapeDtypeStruct((384, 128), F32)),
        in_specs=(free, free),
        out_specs=(free, free),
        scratch_shapes=[pltpu.SemaphoreType.DMA((2,))],
        compiler_params=pltpu.CompilerParams(vmem_limit_bytes=1024 * 1024),
    )(tendency, stress)
    return tendency.reshape(3, 4, 16, 128), stress.reshape(6, 4, 16, 128)


def solution(mesh):
    placed = (P(None, "gx", "gy", None), P(), P(), P())
    return jax.shard_map(
        shards,
        mesh=mesh,
        in_specs=placed,
        out_specs=(P(None, "gx", "gy", None), P(None, "gx", "gy", None)),
        check_vma=False,
    )
```
